32 devices in a mesh: ctx: 4 (over y, x), exp: 8 (over z, core).
Axes of the slice: x: 2, y: 2, z: 4, core: 2. Of those that a mesh axis runs over, the one named last changes fastest.
Arguments:
- queries: bfloat16 [4096, 2048], P('ctx', 'exp'), may hold values from -6 to 6
- keys: bfloat16 [4096, 2048], P('ctx', 'exp'), may hold values from -6 to 6
- values: bfloat16 [4096, 2048], P('ctx', 'exp'), may hold values from -6 to 6
- gate_input: bfloat16 [4096, 2048], P(('ctx', 'exp')), may hold values from -6 to 6
- route_ids: int32 [4096, 2], P(('ctx', 'exp')), may hold values from 0 to 15, all different within a row; in each aligned block of 128 rows (0 to 127, 128 to 255, ...) at most 32 rows name the same one
- route_gates: float32 [4096, 2], P(('ctx', 'exp')), may hold values from 0.1 to 1
- w_gate: bfloat16 [16, 2048, 512], P('exp'), may hold values from -0.125 to 0.125
- w_up: bfloat16 [16, 2048, 512], P('exp'), may hold values from -0.125 to 0.125
- w_down: bfloat16 [16, 512, 2048], P('exp'), may hold values from -0.25 to 0.25
- out_grad: bfloat16 [4096, 2048], P(('ctx', 'exp')), may hold values from -6 to 6
Outputs:
- normed: bfloat16 [4096, 2048], P(('ctx', 'exp'))
- mixed: bfloat16 [4096, 2048], P(('ctx', 'exp'))
- normed_grad: bfloat16 [4096, 2048], P(('ctx', 'exp'))
- w_gate_grad: bfloat16 [16, 2048, 512], P('exp', 'ctx')
- w_up_grad: bfloat16 [16, 2048, 512], P('exp', 'ctx')
- w_down_grad: bfloat16 [16, 512, 2048], P('exp', None, 'ctx')
The draws below stay inside these ranges and needn't reach their ends.
Inputs may be any that keep to these rules, and one draw needn't show every extreme that they name: `route_ids`: each position names two different experts. Within the 128 positions of one aligned block no expert is named by more than 32 routes, and in every draw some expert is named by exactly 32 routes of some block.
All inputs are finite; a program needn't handle non-finite values.
Results may differ from the reference program's by a relative error of at most 0.013.
Values may be sent and summed in bfloat16 or wider, within the bound.
A program may use at most 128 MiB of HBM per device.

```python
import math
import jax
import jax.numpy as jnp
import numpy as np
from jax import lax

D = 2048
HEAD_DIM = 128
HIDDEN_SIZE = 512
TOK_DEV = 128
HEADS = 16
EXPERTS = 16
CAP = 32
SEQ = 4096
N_CTX = 4
N_EXP = 8


def block_scale(rng, dims, cuts, smallest, top_value):
    loudness = 1.0
    for position, parts in cuts:
        steps = jax.random.uniform(jax.random.fold_in(jax.random.fold_in(rng, 6), position), (parts,), jnp.float32, smallest / len(cuts), top_value / len(cuts))
        loudness = loudness * jnp.repeat(jnp.exp(steps), dims[position] // parts).reshape((-1,) + (1,) * (len(dims) - 1 - position))
    return loudness


def assign_block(key, own, number, rows, count, top, reach, lean):
    order = jax.random.permutation(key, count)
    heavy_load, ordinary = portions_of(count, rows * top, reach, lean, True), portions_of(count, rows * top, reach, lean, False)
    places = jnp.arange(count)

    def named(sizes, turn):
        used = int((sizes > 0).sum())
        fixed = max(1, used // 4)
        moved = fixed + (places - fixed + turn * (used - fixed)) % max(1, count - fixed)
        return jnp.zeros((count,), jnp.int32).at[order[jnp.where(places < fixed, places, moved)]].set(jnp.asarray(sizes, jnp.int32))

    sizes = jnp.where(number % 4 == 0, named(heavy_load, number // 4), named(ordinary, number - number // 4 - 1))
    mixed = jax.random.permutation(jax.random.fold_in(own, 3), count)
    giver, taker = mixed[0:count // 2 * 2:2], mixed[1:count // 2 * 2:2]
    margin = jnp.minimum(sizes[giver] - 1, reach - sizes[taker]) // 2
    margin = jnp.where((giver == order[0]) | (taker == order[0]) | (sizes[taker] == 0), 0, jnp.maximum(margin, 0))
    moved = jax.random.randint(jax.random.fold_in(own, 4), (count // 2,), 0, 1 << 20) % (margin + 1)
    sizes = sizes.at[giver].add(-moved).at[taker].add(moved)
    items = jnp.searchsorted(jnp.cumsum(sizes), jnp.arange(rows * top), side="right").astype(jnp.int32)
    table = items.reshape(top, rows).T
    table = table[jax.random.permutation(jax.random.fold_in(own, 1), rows)]
    turn = jax.random.randint(jax.random.fold_in(own, 2), (rows, 1), 0, top)
    return jnp.take_along_axis(table, (jnp.arange(top)[None, :] + turn) % top, axis=1)


def portions_of(number_of, total, most, slope, full):
    portions = [(1 << 20) // math.isqrt(standing ** slope) + 1 for standing in range(1, number_of + 1)]
    largest = most if full else min(most, max(-(-total // number_of), total * portions[0] // sum(portions)))
    least = 1 if total - largest >= number_of - 1 else 0
    holding, surplus = [largest] + [least] * (number_of - 1), total - largest - least * (number_of - 1)
    while surplus > 0:
        movable = [i for i in range(1, number_of) if holding[i] < largest] or [i for i in range(1, number_of) if holding[i] < most]
        pool, left = sum([portions[i] for i in movable]), surplus
        for i in movable:
            extra = min(most - holding[i], max(1, left * portions[i] // pool), surplus)
            holding[i] = holding[i] + extra
            surplus = surplus - extra
    return np.array(holding)


def scatter_about(rng, shape, scale, most, pieces=(), kind=jnp.bfloat16):
    array = jax.random.normal(rng, shape, jnp.float32) * scale
    if len(pieces) > 0:
        array = block_scale(rng, shape, pieces, -0.22, 0.18) * array
    return jnp.clip(array, min=-most, max=most).astype(kind)


def setup_inputs(seed: int = 0) -> dict:
    splits = jax.random.split(jax.random.key(seed), 11)
    queries = scatter_about(splits[0], (SEQ, D), 1.0, 6.0, ((0, 4), (1, 8)))
    keys = scatter_about(splits[1], (SEQ, D), 1.0, 6.0, ((0, 4), (1, 8)))
    values = scatter_about(splits[2], (SEQ, D), 1.0, 6.0, ((0, 4), (1, 8)))
    gate_input = scatter_about(splits[3], (SEQ, D), 1.0, 6.0, ((0, 32),))
    route_ids_keys = jax.random.split(jax.random.fold_in(splits[4], 1), SEQ // TOK_DEV)
    route_ids_turns = jax.random.permutation(jax.random.fold_in(splits[4], 3), SEQ // TOK_DEV)
    route_ids = jax.vmap(lambda own, number: assign_block(jax.random.fold_in(splits[4], 2), own, number, TOK_DEV, EXPERTS, 2, CAP, 2))(route_ids_keys, route_ids_turns).reshape((SEQ, 2))
    route_gates = jnp.clip(0.1 + 0.9 * jax.random.uniform(splits[5], (SEQ, 2), jnp.float32) ** block_scale(splits[5], (SEQ, 2), ((0, 32),), -0.2, 0.2), 0.1, 1.0)
    w_gate = scatter_about(splits[6], (EXPERTS, D, HIDDEN_SIZE), D ** -0.5, 0.125, ((0, 8),))
    w_up = scatter_about(splits[7], (EXPERTS, D, HIDDEN_SIZE), D ** -0.5, 0.125, ((0, 8),))
    w_down = scatter_about(splits[8], (EXPERTS, HIDDEN_SIZE, D), HIDDEN_SIZE ** -0.5, 0.25, ((0, 8),))
    out_grad = scatter_about(splits[9], (SEQ, D), 1.0, 6.0, ((0, 32),))
    return dict(queries=queries, keys=keys, values=values, gate_input=gate_input, route_ids=route_ids, route_gates=route_gates, w_gate=w_gate, w_up=w_up, w_down=w_down, out_grad=out_grad)


def silu_grad(value):
    sigma = jax.nn.sigmoid(value)
    return sigma * (1.0 + value * (1.0 - sigma))

def attention(queries, keys, values):
    block_rows = TOK_DEV * N_EXP
    block_count = SEQ // block_rows
    query_heads = queries.reshape(block_count, block_rows, HEADS, HEAD_DIM)
    key_heads = keys.reshape(block_count, block_rows, HEADS, HEAD_DIM)
    value_heads = values.reshape(block_count, block_rows, HEADS, HEAD_DIM)
    scale = 1.0 / math.sqrt(HEAD_DIM)
    positions = jnp.arange(block_rows, dtype=jnp.int32)

    def one_query(query_index):
        query_block = lax.dynamic_index_in_dim(query_heads, query_index, 0, keepdims=False).astype(jnp.float32)

        def over_keys(running, key_index):

            def compute(inner):
                key_block = lax.dynamic_index_in_dim(key_heads, key_index, 0, keepdims=False).astype(jnp.float32)
                value_block = lax.dynamic_index_in_dim(value_heads, key_index, 0, keepdims=False).astype(jnp.float32)
                scores = jnp.einsum('qhd,khd->hqk', query_block, key_block) * scale
                allowed = (query_index * block_rows + positions)[:, None] >= (key_index * block_rows + positions)[None, :]
                weight = jnp.where(allowed[None], jax.nn.silu(scores), 0.0).astype(jnp.bfloat16)
                weight = lax.optimization_barrier(weight).astype(jnp.float32)
                return inner + jnp.einsum('hqk,khd->qhd', weight, value_block)
            return (lax.cond(key_index <= query_index, compute, lambda inner: inner, running), None)
        initial = jnp.zeros((block_rows, HEADS, HEAD_DIM), jnp.float32)
        result, unused = lax.scan(over_keys, initial, jnp.arange(block_count, dtype=jnp.int32))
        return result
    blocks = lax.map(one_query, jnp.arange(block_count, dtype=jnp.int32))
    return blocks.reshape(SEQ, HEADS * HEAD_DIM).astype(jnp.bfloat16)

def group_sum(left, right):
    group_rows = N_EXP * CAP
    left_groups = left.reshape(N_CTX, group_rows, left.shape[1]).astype(jnp.float32)
    right_groups = right.reshape(N_CTX, group_rows, right.shape[1]).astype(jnp.float32)
    partial_terms = jnp.einsum('crd,crh->cdh', left_groups, right_groups).astype(jnp.bfloat16)
    partial_terms = lax.optimization_barrier(partial_terms).astype(jnp.float32)
    return lax.optimization_barrier(jnp.sum(partial_terms, axis=0)).astype(jnp.bfloat16)

def reference(queries, keys, values, gate_input, route_ids, route_gates, w_gate, w_up, w_down, out_grad):
    attended = attention(queries, keys, values).astype(jnp.float32)
    mean_rows = lax.optimization_barrier(jnp.mean(attended, axis=1, keepdims=True))
    centred = attended - mean_rows
    variance = lax.optimization_barrier(jnp.mean(centred * centred, axis=1, keepdims=True))
    normed = (centred * lax.rsqrt(variance + 1e-05) * gate_input.astype(jnp.float32)).astype(jnp.bfloat16)
    block_count = SEQ // TOK_DEV
    flat_ids = route_ids.reshape(block_count, TOK_DEV * 2)
    onehot = (flat_ids[:, :, None] == jnp.arange(EXPERTS, dtype=jnp.int32)[None, None, :]).astype(jnp.int32)
    slot_ids = lax.optimization_barrier(jnp.sum((jnp.cumsum(onehot, axis=1) - onehot) * onehot, axis=2))
    row_ids = (jnp.arange(block_count, dtype=jnp.int32)[:, None] * CAP + slot_ids).reshape(-1).astype(jnp.int32)
    expert_ids = flat_ids.reshape(-1).astype(jnp.int32)
    buffer_rows = block_count * CAP

    def scatter_rows(source_rows):
        return jnp.zeros((EXPERTS, buffer_rows, D), jnp.bfloat16).at[expert_ids, row_ids].set(source_rows)
    expert_inputs = scatter_rows(jnp.repeat(normed, 2, axis=0))
    scaled_grad = (route_gates[:, :, None] * out_grad.astype(jnp.float32)[:, None, :]).astype(jnp.bfloat16)
    expert_grads = scatter_rows(scaled_grad.reshape(SEQ * 2, D))

    def one_expert(items):
        inputs, grads, gate_weight, up_weight, down_weight = items
        gate_pre = jnp.dot(inputs, gate_weight, preferred_element_type=jnp.float32)
        up_pre = jnp.dot(inputs, up_weight, preferred_element_type=jnp.float32)
        hidden = (jax.nn.silu(gate_pre) * up_pre).astype(jnp.bfloat16)
        output = jnp.dot(hidden, down_weight, preferred_element_type=jnp.float32).astype(jnp.bfloat16)
        hidden_grad = jnp.dot(grads, down_weight.T, preferred_element_type=jnp.float32)
        gate_grad = (hidden_grad * up_pre * silu_grad(gate_pre)).astype(jnp.bfloat16)
        up_grad = (hidden_grad * jax.nn.silu(gate_pre)).astype(jnp.bfloat16)
        input_grad = (jnp.dot(gate_grad, gate_weight.T, preferred_element_type=jnp.float32) + jnp.dot(up_grad, up_weight.T, preferred_element_type=jnp.float32)).astype(jnp.bfloat16)
        gate_wgrad = group_sum(inputs, gate_grad)
        up_wgrad = group_sum(inputs, up_grad)
        down_wgrad = group_sum(hidden, grads)
        return (output, input_grad, gate_wgrad, up_wgrad, down_wgrad)
    outputs, input_grads, gate_wgrads, up_wgrads, down_wgrads = lax.map(one_expert, (expert_inputs, expert_grads, w_gate, w_up, w_down))
    picked = outputs[expert_ids, row_ids].reshape(SEQ, 2, D).astype(jnp.float32)
    mixed = lax.optimization_barrier(jnp.sum(picked * route_gates[:, :, None], axis=1)).astype(jnp.bfloat16)
    picked_grads = input_grads[expert_ids, row_ids].reshape(SEQ, 2, D).astype(jnp.float32)
    normed_grad = lax.optimization_barrier(jnp.sum(picked_grads, axis=1)).astype(jnp.bfloat16)
    return (normed, mixed, normed_grad, gate_wgrads, up_wgrads, down_wgrads)
```

```python
import functools
import math

import jax
import jax.numpy as jnp
from jax import lax
from jax.experimental import pallas as pl
from jax.experimental.pallas import tpu as pltpu
from jax.sharding import PartitionSpec as P

HEAD_DIM = 128
NT = (((1,), (1,)), ((), ()))


def silu_grad(value):
    sigma = jax.nn.sigmoid(value)
    return sigma * (1.0 + value * (1.0 - sigma))


def weigh(query, key, half_scale):
    half = lax.dot_general(query, key, NT, preferred_element_type=jnp.float32) * half_scale
    return half + half * jnp.tanh(half)


def own_kernel(half_scale, chunks, q_ref, k_ref, v_ref, o_ref):
    rows = q_ref.shape[0]
    step = pl.program_id(1)
    query = q_ref[...]
    keep = lax.broadcasted_iota(jnp.int32, (rows, rows), 0) >= lax.broadcasted_iota(
        jnp.int32, (rows, rows), 1
    )
    start = pl.multiple_of(step * rows, rows)
    weight = jnp.where(keep, weigh(query, k_ref[pl.ds(start, rows), :], half_scale), 0.0)
    o_ref[...] = jnp.dot(
        weight.astype(jnp.bfloat16),
        v_ref[pl.ds(start, rows), :],
        preferred_element_type=jnp.float32,
    )
    for chunk in range(chunks - 1):

        @pl.when(chunk < step)
        def _(chunk=chunk):
            part = slice(chunk * rows, (chunk + 1) * rows)
            weight = weigh(query, k_ref[part, :], half_scale)
            o_ref[...] += jnp.dot(
                weight.astype(jnp.bfloat16), v_ref[part, :], preferred_element_type=jnp.float32
            )


def earlier_kernel(half_scale, slots, part_rows, q_ref, own_ref, *refs):
    o_ref, acc_ref = refs[2 * slots], refs[2 * slots + 1]
    here = lax.axis_index("ctx")
    query = q_ref[...]
    acc_ref[...] = own_ref[...]
    for slot in range(slots):

        @pl.when(here > slot)
        def _(slot=slot):
            k_ref, v_ref = refs[2 * slot], refs[2 * slot + 1]
            total = jnp.zeros(acc_ref.shape, jnp.float32)
            for first in range(0, k_ref.shape[0], part_rows):
                part = slice(first, first + part_rows)
                weight = weigh(query, k_ref[part, :], half_scale)
                total += jnp.dot(
                    weight.astype(jnp.bfloat16), v_ref[part, :], preferred_element_type=jnp.float32
                )
            acc_ref[...] += total

    o_ref[...] = acc_ref[...].astype(o_ref.dtype)


def attend_own(queries, keys, values):
    rows, cols = queries.shape
    block = min(rows, 256)
    grid = (cols // HEAD_DIM, rows // block)
    whole = pl.BlockSpec((rows, HEAD_DIM), lambda h, i: (0, h))
    piece = pl.BlockSpec((block, HEAD_DIM), lambda h, i: (i, h))
    return pl.pallas_call(
        functools.partial(own_kernel, 0.5 / math.sqrt(HEAD_DIM), rows // block),
        grid=grid,
        out_shape=jax.ShapeDtypeStruct((rows, cols), jnp.float32),
        in_specs=[piece, whole, whole],
        out_specs=piece,
        compiler_params=pltpu.CompilerParams(vmem_limit_bytes=24 * 2**20),
        cost_estimate=pl.CostEstimate(
            flops=4 * rows * rows * cols, bytes_accessed=10 * rows * cols, transcendentals=0
        ),
    )(queries, keys, values)


def attend_earlier(queries, own, pairs):
    rows, cols = queries.shape
    block = min(rows, 256)
    grid = (cols // HEAD_DIM, rows // block)
    whole = pl.BlockSpec((rows, HEAD_DIM), lambda h, i: (0, h))
    piece = pl.BlockSpec((block, HEAD_DIM), lambda h, i: (i, h))
    flat = [item for pair in pairs for item in pair]
    return pl.pallas_call(
        functools.partial(earlier_kernel, 0.5 / math.sqrt(HEAD_DIM), len(pairs), min(rows, 512)),
        grid=grid,
        out_shape=jax.ShapeDtypeStruct((rows, cols), jnp.bfloat16),
        in_specs=[piece, piece] + [whole] * len(flat),
        out_specs=piece,
        scratch_shapes=[pltpu.VMEM((block, HEAD_DIM), jnp.float32)],
        compiler_params=pltpu.CompilerParams(vmem_limit_bytes=32 * 2**20),
        cost_estimate=pl.CostEstimate(
            flops=4 * rows * rows * cols * len(pairs),
            bytes_accessed=2 * rows * cols * (4 + len(flat)),
            transcendentals=0,
        ),
    )(queries, own, *flat)


def earlier_shards(keys, values, count):
    if count != 4:
        return [
            tuple(
                lax.ppermute(x, "ctx", [(i, i + shift) for i in range(count - shift)])
                for x in (keys, values)
            )
            for shift in range(1, count)
        ]
    here = lax.axis_index("ctx")
    along_a = [lax.ppermute(x, "ctx", [(0, 1), (2, 3)]) for x in (keys, values)]
    along_b = [lax.ppermute(x, "ctx", [(0, 2), (1, 3)]) for x in (keys, values)]
    first = [jnp.where(here == 1, a, b) for a, b in zip(along_a, along_b)]
    second = (
        lax.ppermute(first[0], "ctx", [(1, 3), (3, 2)]),
        lax.ppermute(first[1], "ctx", [(2, 3), (3, 2)]),
    )
    return [tuple(first), second, tuple(along_a)]


def swap(value, step, count):
    return lax.ppermute(value, "ctx", [(i, i ^ step) for i in range(count)])


def body(queries, keys, values, gate_input, route_ids, route_gates, w_gate, w_up, w_down, out_grad):
    ctx = lax.axis_size("ctx")
    here = lax.axis_index("ctx")
    tok_rows, width = out_grad.shape
    experts = lax.axis_size("exp") * w_gate.shape[0]
    capacity = 4 * tok_rows // experts

    flat_ids = route_ids.reshape(-1)
    routes = flat_ids.shape[0]
    onehot = flat_ids[:, None] == jnp.arange(experts, dtype=jnp.int32)[None, :]
    order = jnp.arange(routes, dtype=jnp.int32)
    before = (order[:, None] > order[None, :]).astype(jnp.bfloat16)
    earlier = jnp.dot(before, onehot.astype(jnp.bfloat16), preferred_element_type=jnp.float32)
    slot_ids = jnp.sum(jnp.where(onehot, earlier, 0.0), axis=1).astype(jnp.int32)
    dest = (flat_ids * capacity + slot_ids).reshape(tok_rows, 2)
    buffer = jnp.arange(experts * capacity, dtype=jnp.int32)
    hit0 = dest[:, 0][None, :] == buffer[:, None]
    hit1 = dest[:, 1][None, :] == buffer[:, None]
    place = (hit0 | hit1).astype(jnp.bfloat16)
    gates0, gates1 = route_gates[:, 0][None, :], route_gates[:, 1][None, :]
    gate_table = jnp.where(hit0, gates0, 0.0) + jnp.where(hit1, gates1, 0.0)
    row_gate = jnp.sum(gate_table, axis=1)

    picked_grad = jnp.dot(place, out_grad, preferred_element_type=jnp.float32)
    send_grads = (
        (picked_grad * row_gate[:, None]).astype(jnp.bfloat16).reshape(experts, capacity, width)
    )
    recv_grads = lax.all_to_all(send_grads, "exp", split_axis=0, concat_axis=1, tiled=True)

    pairs = earlier_shards(keys, values, ctx)
    own = attend_own(queries, keys, values)
    attended = attend_earlier(queries, own, pairs)
    attended, recv_grads = lax.optimization_barrier((attended, recv_grads))
    token_rows = lax.all_to_all(
        attended, "exp", split_axis=0, concat_axis=1, tiled=True
    ).astype(jnp.float32)
    mean_rows = jnp.mean(token_rows, axis=1, keepdims=True)
    centred = token_rows - mean_rows
    variance = jnp.mean(centred * centred, axis=1, keepdims=True)
    normed = (centred * lax.rsqrt(variance + 1e-05) * gate_input.astype(jnp.float32)).astype(
        jnp.bfloat16
    )
    send_inputs = (
        jnp.dot(place, normed, preferred_element_type=jnp.float32)
        .astype(jnp.bfloat16)
        .reshape(experts, capacity, width)
    )
    recv_inputs = lax.all_to_all(send_inputs, "exp", split_axis=0, concat_axis=1, tiled=True)

    share = width // ctx

    def share_of(value, owner):
        return lax.dynamic_slice_in_dim(value, owner * share, share, 2)

    grad_shares = [share_of(recv_grads, here)] + [
        swap(share_of(recv_grads, here ^ step), step, ctx) for step in range(1, ctx)
    ]
    hidden_grad = jnp.einsum("erd,ehd->erh", recv_grads, w_down, preferred_element_type=jnp.float32)

    gate_pre = jnp.einsum("erd,edh->erh", recv_inputs, w_gate, preferred_element_type=jnp.float32)
    up_pre = jnp.einsum("erd,edh->erh", recv_inputs, w_up, preferred_element_type=jnp.float32)
    hidden = (jax.nn.silu(gate_pre) * up_pre).astype(jnp.bfloat16)
    expert_out = jnp.einsum(
        "erh,ehd->erd", hidden, w_down, preferred_element_type=jnp.float32
    ).astype(jnp.bfloat16)
    back_out = lax.all_to_all(expert_out, "exp", split_axis=1, concat_axis=0, tiled=True)
    gate_grad = (hidden_grad * up_pre * silu_grad(gate_pre)).astype(jnp.bfloat16)
    up_grad = (hidden_grad * jax.nn.silu(gate_pre)).astype(jnp.bfloat16)
    input_grad = (
        jnp.einsum("erh,edh->erd", gate_grad, w_gate, preferred_element_type=jnp.float32)
        + jnp.einsum("erh,edh->erd", up_grad, w_up, preferred_element_type=jnp.float32)
    ).astype(jnp.bfloat16)
    back_grad = lax.all_to_all(input_grad, "exp", split_axis=1, concat_axis=0, tiled=True)

    gate_sum = up_sum = down_sum = 0.0
    for step in range(ctx):
        inputs = share_of(recv_inputs, here ^ step)
        acts = (hidden, gate_grad, up_grad)
        if step:
            inputs = swap(inputs, step, ctx)
            acts = tuple(swap(act, step, ctx) for act in acts)
        partials = (
            jnp.einsum("erd,erh->edh", inputs, acts[1], preferred_element_type=jnp.float32),
            jnp.einsum("erd,erh->edh", inputs, acts[2], preferred_element_type=jnp.float32),
            jnp.einsum("erh,erd->ehd", acts[0], grad_shares[step], preferred_element_type=jnp.float32),
        )
        gate_part, up_part, down_part = (
            x.astype(jnp.bfloat16).astype(jnp.float32) for x in partials
        )
        gate_sum, up_sum, down_sum = gate_sum + gate_part, up_sum + up_part, down_sum + down_part

    gate_high = lax.reduce_precision(gate_table, 8, 7)
    gate_parts = jnp.concatenate([gate_high, gate_table - gate_high], axis=1).astype(jnp.bfloat16)
    into = (((0,), (0,)), ((), ()))
    both = lax.dot_general(
        gate_parts,
        back_out.reshape(experts * capacity, width),
        into,
        preferred_element_type=jnp.float32,
    )
    mixed = (both[:tok_rows] + both[tok_rows:]).astype(jnp.bfloat16)
    normed_grad = lax.dot_general(
        place,
        back_grad.reshape(experts * capacity, width),
        into,
        preferred_element_type=jnp.float32,
    ).astype(jnp.bfloat16)
    return (
        normed,
        mixed,
        normed_grad,
        gate_sum.astype(jnp.bfloat16),
        up_sum.astype(jnp.bfloat16),
        down_sum.astype(jnp.bfloat16),
    )


def solution(mesh):
    in_specs = (
        P("ctx", "exp"),
        P("ctx", "exp"),
        P("ctx", "exp"),
        P(("ctx", "exp"), None),
        P(("ctx", "exp"), None),
        P(("ctx", "exp"), None),
        P("exp", None, None),
        P("exp", None, None),
        P("exp", None, None),
        P(("ctx", "exp"), None),
    )
    out_specs = (
        P(("ctx", "exp"), None),
        P(("ctx", "exp"), None),
        P(("ctx", "exp"), None),
        P("exp", "ctx", None),
        P("exp", "ctx", None),
        P("exp", None, "ctx"),
    )
    return jax.shard_map(body, mesh=mesh, in_specs=in_specs, out_specs=out_specs, check_vma=False)
```

```python
import functools
import math

import jax
import jax.numpy as jnp
from jax import lax
from jax.experimental import pallas as pl
from jax.experimental.pallas import tpu as pltpu
from jax.sharding import PartitionSpec as P

HEAD_DIM = 128
NT = (((1,), (1,)), ((), ()))


def silu_grad(value):
    sigma = jax.nn.sigmoid(value)
    return sigma * (1.0 + value * (1.0 - sigma))


def weigh(query, key, half_scale):
    half = lax.dot_general(query, key, NT, preferred_element_type=jnp.float32) * half_scale
    return half + half * jnp.tanh(half)


def own_kernel(half_scale, chunks, q_ref, k_ref, v_ref, o_ref):
    rows = q_ref.shape[0]
    step = pl.program_id(1)
    query = q_ref[...]
    keep = lax.broadcasted_iota(jnp.int32, (rows, rows), 0) >= lax.broadcasted_iota(
        jnp.int32, (rows, rows), 1
    )
    start = pl.multiple_of(step * rows, rows)
    weight = jnp.where(keep, weigh(query, k_ref[pl.ds(start, rows), :], half_scale), 0.0)
    o_ref[...] = jnp.dot(
        weight.astype(jnp.bfloat16),
        v_ref[pl.ds(start, rows), :],
        preferred_element_type=jnp.float32,
    )
    for chunk in range(chunks - 1):

        @pl.when(chunk < step)
        def _(chunk=chunk):
            part = slice(chunk * rows, (chunk + 1) * rows)
            weight = weigh(query, k_ref[part, :], half_scale)
            o_ref[...] += jnp.dot(
                weight.astype(jnp.bfloat16), v_ref[part, :], preferred_element_type=jnp.float32
            )


def earlier_kernel(half_scale, slots, part_rows, q_ref, own_ref, *refs):
    o_ref, acc_ref = refs[2 * slots], refs[2 * slots + 1]
    here = lax.axis_index("ctx")
    query = q_ref[...]
    acc_ref[...] = own_ref[...]
    for slot in range(slots):

        @pl.when(here > slot)
        def _(slot=slot):
            k_ref, v_ref = refs[2 * slot], refs[2 * slot + 1]
            total = jnp.zeros(acc_ref.shape, jnp.float32)
            for first in range(0, k_ref.shape[0], part_rows):
                part = slice(first, first + part_rows)
                weight = weigh(query, k_ref[part, :], half_scale)
                total += jnp.dot(
                    weight.astype(jnp.bfloat16), v_ref[part, :], preferred_element_type=jnp.float32
                )
            acc_ref[...] += total

    o_ref[...] = acc_ref[...].astype(o_ref.dtype)


def attend_own(queries, keys, values):
    rows, cols = queries.shape
    block = min(rows, 256)
    grid = (cols // HEAD_DIM, rows // block)
    whole = pl.BlockSpec((rows, HEAD_DIM), lambda h, i: (0, h))
    piece = pl.BlockSpec((block, HEAD_DIM), lambda h, i: (i, h))
    return pl.pallas_call(
        functools.partial(own_kernel, 0.5 / math.sqrt(HEAD_DIM), rows // block),
        grid=grid,
        out_shape=jax.ShapeDtypeStruct((rows, cols), jnp.float32),
        in_specs=[piece, whole, whole],
        out_specs=piece,
        compiler_params=pltpu.CompilerParams(vmem_limit_bytes=24 * 2**20),
        cost_estimate=pl.CostEstimate(
            flops=4 * rows * rows * cols, bytes_accessed=10 * rows * cols, transcendentals=0
        ),
    )(queries, keys, values)


def attend_earlier(queries, own, pairs):
    rows, cols = queries.shape
    block = min(rows, 256)
    grid = (cols // HEAD_DIM, rows // block)
    whole = pl.BlockSpec((rows, HEAD_DIM), lambda h, i: (0, h))
    piece = pl.BlockSpec((block, HEAD_DIM), lambda h, i: (i, h))
    flat = [item for pair in pairs for item in pair]
    return pl.pallas_call(
        functools.partial(earlier_kernel, 0.5 / math.sqrt(HEAD_DIM), len(pairs), min(rows, 512)),
        grid=grid,
        out_shape=jax.ShapeDtypeStruct((rows, cols), jnp.bfloat16),
        in_specs=[piece, piece] + [whole] * len(flat),
        out_specs=piece,
        scratch_shapes=[pltpu.VMEM((block, HEAD_DIM), jnp.float32)],
        compiler_params=pltpu.CompilerParams(vmem_limit_bytes=32 * 2**20),
        cost_estimate=pl.CostEstimate(
            flops=4 * rows * rows * cols * len(pairs),
            bytes_accessed=2 * rows * cols * (4 + len(flat)),
            transcendentals=0,
        ),
    )(queries, own, *flat)


def earlier_shards(keys, values, count):
    if count != 4:
        return [
            tuple(
                lax.ppermute(x, "ctx", [(i, i + shift) for i in range(count - shift)])
                for x in (keys, values)
            )
            for shift in range(1, count)
        ]
    here = lax.axis_index("ctx")
    along_a = [lax.ppermute(x, "ctx", [(0, 1), (2, 3)]) for x in (keys, values)]
    along_b = [lax.ppermute(x, "ctx", [(0, 2), (1, 3)]) for x in (keys, values)]
    first = [jnp.where(here == 1, a, b) for a, b in zip(along_a, along_b)]
    second = (
        lax.ppermute(first[0], "ctx", [(1, 3), (3, 2)]),
        lax.ppermute(first[1], "ctx", [(2, 3), (3, 2)]),
    )
    return [tuple(first), second, tuple(along_a)]


def shift(value, step, count):
    return lax.ppermute(value, "ctx", [(i, (i + step) % count) for i in range(count)])


def exchange_kernel(count, share, sliced, kept, *refs):
    total = sliced + kept
    sources, landed = refs[:total], refs[total : total * count]
    send_sem, recv_sem = refs[total * count :]
    here = lax.axis_index("ctx")
    barrier = pltpu.get_barrier_semaphore()
    for step in range(1, count):
        pl.semaphore_signal(
            barrier,
            inc=1,
            device_id={"ctx": lax.rem(here + step, count)},
            device_id_type=pl.DeviceIdType.MESH,
        )
    pl.semaphore_wait(barrier, count - 1)
    copies = []
    for step in range(1, count):
        owner = lax.rem(here + step, count)
        for item in range(total):
            source = sources[item]
            if item < sliced:
                source = source.at[:, :, pl.ds(pl.multiple_of(owner * share, share), share)]
            place = item * (count - 1) + step - 1
            copies.append(
                pltpu.make_async_remote_copy(
                    src_ref=source,
                    dst_ref=landed[place],
                    send_sem=send_sem.at[place],
                    recv_sem=recv_sem.at[place],
                    device_id={"ctx": owner},
                    device_id_type=pl.DeviceIdType.MESH,
                )
            )
            copies[-1].start()
    for copy in copies:
        copy.wait()


def exchange(sliced, kept, count, share, number):
    arrays = list(sliced) + list(kept)
    shapes = [
        jax.ShapeDtypeStruct(x.shape[:2] + (share if i < len(sliced) else x.shape[2],), x.dtype)
        for i, x in enumerate(arrays)
        for _ in range(count - 1)
    ]
    moved = sum(math.prod(s.shape) * s.dtype.itemsize for s in shapes)
    landed = pl.pallas_call(
        functools.partial(exchange_kernel, count, share, len(sliced), len(kept)),
        out_shape=shapes,
        in_specs=[pl.BlockSpec(memory_space=pl.ANY)] * len(arrays),
        out_specs=[pl.BlockSpec(memory_space=pl.ANY)] * len(shapes),
        scratch_shapes=[
            pltpu.SemaphoreType.DMA((len(shapes),)),
            pltpu.SemaphoreType.DMA((len(shapes),)),
        ],
        compiler_params=pltpu.CompilerParams(collective_id=number, has_side_effects=True),
        cost_estimate=pl.CostEstimate(flops=0, bytes_accessed=20 * moved, transcendentals=0),
    )(*arrays)
    return [list(landed[i * (count - 1) : (i + 1) * (count - 1)]) for i in range(len(arrays))]


def body(queries, keys, values, gate_input, route_ids, route_gates, w_gate, w_up, w_down, out_grad):
    ctx = lax.axis_size("ctx")
    here = lax.axis_index("ctx")
    tok_rows, width = out_grad.shape
    experts = lax.axis_size("exp") * w_gate.shape[0]
    capacity = 4 * tok_rows // experts

    flat_ids = route_ids.reshape(-1)
    routes = flat_ids.shape[0]
    onehot = flat_ids[:, None] == jnp.arange(experts, dtype=jnp.int32)[None, :]
    order = jnp.arange(routes, dtype=jnp.int32)
    before = (order[:, None] > order[None, :]).astype(jnp.bfloat16)
    earlier = jnp.dot(before, onehot.astype(jnp.bfloat16), preferred_element_type=jnp.float32)
    slot_ids = jnp.sum(jnp.where(onehot, earlier, 0.0), axis=1).astype(jnp.int32)
    dest = (flat_ids * capacity + slot_ids).reshape(tok_rows, 2)
    buffer = jnp.arange(experts * capacity, dtype=jnp.int32)
    hit0 = dest[:, 0][None, :] == buffer[:, None]
    hit1 = dest[:, 1][None, :] == buffer[:, None]
    place = (hit0 | hit1).astype(jnp.bfloat16)
    gates0, gates1 = route_gates[:, 0][None, :], route_gates[:, 1][None, :]
    gate_table = jnp.where(hit0, gates0, 0.0) + jnp.where(hit1, gates1, 0.0)
    row_gate = jnp.sum(gate_table, axis=1)

    picked_grad = jnp.dot(place, out_grad, preferred_element_type=jnp.float32)
    send_grads = (
        (picked_grad * row_gate[:, None]).astype(jnp.bfloat16).reshape(experts, capacity, width)
    )
    recv_grads = lax.all_to_all(send_grads, "exp", split_axis=0, concat_axis=1, tiled=True)

    pairs = earlier_shards(keys, values, ctx)
    own = attend_own(queries, keys, values)
    attended = attend_earlier(queries, own, pairs)
    attended, recv_grads = lax.optimization_barrier((attended, recv_grads))
    token_rows = lax.all_to_all(
        attended, "exp", split_axis=0, concat_axis=1, tiled=True
    ).astype(jnp.float32)
    mean_rows = jnp.mean(token_rows, axis=1, keepdims=True)
    centred = token_rows - mean_rows
    variance = jnp.mean(centred * centred, axis=1, keepdims=True)
    normed = (centred * lax.rsqrt(variance + 1e-05) * gate_input.astype(jnp.float32)).astype(
        jnp.bfloat16
    )
    send_inputs = (
        jnp.dot(place, normed, preferred_element_type=jnp.float32)
        .astype(jnp.bfloat16)
        .reshape(experts, capacity, width)
    )
    recv_inputs = lax.all_to_all(send_inputs, "exp", split_axis=0, concat_axis=1, tiled=True)

    share = width // ctx

    def share_of(value, step):
        return lax.dynamic_slice_in_dim(value, (here + step) % ctx * share, share, 2)

    grad_shares = [share_of(recv_grads, 0)] + [
        shift(share_of(recv_grads, step), step, ctx) for step in range(1, ctx)
    ]
    hidden_grad = jnp.einsum("erd,ehd->erh", recv_grads, w_down, preferred_element_type=jnp.float32)
    recv_inputs, grad_shares, hidden_grad = lax.optimization_barrier(
        (recv_inputs, grad_shares, hidden_grad)
    )

    def send_back(value):
        local = value.shape[0]
        turned = value.reshape(local, experts // local, capacity, width).transpose(1, 0, 2, 3)
        return lax.all_to_all(turned, "exp", split_axis=0, concat_axis=0, tiled=True)

    gate_pre = jnp.einsum("erd,edh->erh", recv_inputs, w_gate, preferred_element_type=jnp.float32)
    up_pre = jnp.einsum("erd,edh->erh", recv_inputs, w_up, preferred_element_type=jnp.float32)
    hidden = (jax.nn.silu(gate_pre) * up_pre).astype(jnp.bfloat16)
    expert_out = jnp.einsum(
        "erh,ehd->erd", hidden, w_down, preferred_element_type=jnp.float32
    ).astype(jnp.bfloat16)
    back_out = send_back(expert_out)
    gate_grad = (hidden_grad * up_pre * silu_grad(gate_pre)).astype(jnp.bfloat16)
    up_grad = (hidden_grad * jax.nn.silu(gate_pre)).astype(jnp.bfloat16)
    input_grad = (
        jnp.einsum("erh,edh->erd", gate_grad, w_gate, preferred_element_type=jnp.float32)
        + jnp.einsum("erh,edh->erd", up_grad, w_up, preferred_element_type=jnp.float32)
    ).astype(jnp.bfloat16)
    inputs_there, hiddens_there = exchange([recv_inputs], [hidden], ctx, share, 1)
    input_shares = [share_of(recv_inputs, 0)] + inputs_there
    hiddens = [hidden] + hiddens_there
    back_out, input_grad, gate_grad, up_grad, hiddens = lax.optimization_barrier(
        (back_out, input_grad, gate_grad, up_grad, hiddens)
    )
    back_grad = send_back(input_grad)
    gates_there, ups_there = exchange([], [gate_grad, up_grad], ctx, share, 2)
    gate_grads = [gate_grad] + gates_there
    up_grads = [up_grad] + ups_there
    gate_sum = up_sum = down_sum = 0.0
    for step in range(ctx):
        partials = (
            jnp.einsum("erd,erh->edh", input_shares[step], gate_grads[step], preferred_element_type=jnp.float32),
            jnp.einsum("erd,erh->edh", input_shares[step], up_grads[step], preferred_element_type=jnp.float32),
            jnp.einsum("erh,erd->ehd", hiddens[step], grad_shares[step], preferred_element_type=jnp.float32),
        )
        gate_part, up_part, down_part = (
            x.astype(jnp.bfloat16).astype(jnp.float32) for x in partials
        )
        gate_sum, up_sum, down_sum = gate_sum + gate_part, up_sum + up_part, down_sum + down_part

    gate_high = lax.reduce_precision(gate_table, 8, 7)
    gate_parts = jnp.concatenate([gate_high, gate_table - gate_high], axis=1).astype(jnp.bfloat16)
    into = (((0,), (0,)), ((), ()))
    both = lax.dot_general(
        gate_parts,
        back_out.reshape(experts * capacity, width),
        into,
        preferred_element_type=jnp.float32,
    )
    mixed = (both[:tok_rows] + both[tok_rows:]).astype(jnp.bfloat16)
    normed_grad = lax.dot_general(
        place,
        back_grad.reshape(experts * capacity, width),
        into,
        preferred_element_type=jnp.float32,
    ).astype(jnp.bfloat16)
    return (
        normed,
        mixed,
        normed_grad,
        gate_sum.astype(jnp.bfloat16),
        up_sum.astype(jnp.bfloat16),
        down_sum.astype(jnp.bfloat16),
    )


def solution(mesh):
    in_specs = (
        P("ctx", "exp"),
        P("ctx", "exp"),
        P("ctx", "exp"),
        P(("ctx", "exp"), None),
        P(("ctx", "exp"), None),
        P(("ctx", "exp"), None),
        P("exp", None, None),
        P("exp", None, None),
        P("exp", None, None),
        P(("ctx", "exp"), None),
    )
    out_specs = (
        P(("ctx", "exp"), None),
        P(("ctx", "exp"), None),
        P(("ctx", "exp"), None),
        P("exp", "ctx", None),
        P("exp", "ctx", None),
        P("exp", None, "ctx"),
    )
    return jax.shard_map(body, mesh=mesh, in_specs=in_specs, out_specs=out_specs, check_vma=False)
```
